32 devices in a mesh: rows: 8 (over z, x), cols: 4 (over y, core).
Axes of the slice: x: 2, y: 2, z: 4, core: 2. Of those that a mesh axis runs over, the one named last changes fastest.
Arguments:
- features: bfloat16 [768, 128, 512], P(None, 'rows', 'cols'), may hold values from -6 to 6
- labels: int32 [128, 512], P('rows', 'cols'), may hold values from 0 to 15
- w_input: bfloat16 [128, 768], replicated, may hold values from -0.21875 to 0.21875
- w_dilate4: bfloat16 [128, 1152], replicated, may hold values from -0.1875 to 0.1875
- w_dilate8: bfloat16 [128, 1152], replicated, may hold values from -0.1875 to 0.1875
- w_classes: bfloat16 [16, 128], replicated, may hold values from -0.5 to 0.5
Outputs:
- grad_input: float32 [128, 768], replicated
- grad_dilate4: float32 [128, 1152], replicated
- grad_dilate8: float32 [128, 1152], replicated
- grad_classes: float32 [16, 128], replicated
The draws below stay inside these ranges and needn't reach their ends.
All inputs are finite; a program needn't handle non-finite values.
Results may differ from the reference program's by a relative error of at most 0.006.
Values may be sent and summed in bfloat16 or wider, within the bound.
A program may use at most 128 MiB of HBM per device.

```python
import jax
import jax.numpy as jnp
from jax import lax

CH = 768
MID = 128
CLASSES = 16
HEIGHT = 128
WIDTH = 512


def plant(result, rng, least, largest):
    place = [jax.random.randint(jax.random.fold_in(rng, axis), (), 0, length) for axis, length in enumerate(result.shape)]
    main_axis = result.shape.index(max(result.shape))
    beside = place[:main_axis] + [(place[main_axis] + 1) % result.shape[main_axis]] + place[main_axis + 1:]
    return result.at[tuple(place)].set(least).at[tuple(beside)].set(largest)


def level_of(stream_key, dims, cuts, least, largest):
    loudness = 1.0
    for position, shards_of in cuts:
        draws = jax.random.uniform(jax.random.fold_in(jax.random.fold_in(stream_key, 6), position), (shards_of,), jnp.float32, least / len(cuts), largest / len(cuts))
        loudness = loudness * jnp.repeat(jnp.exp(draws), dims[position] // shards_of).reshape((-1,) + (1,) * (len(dims) - 1 - position))
    return loudness


def bell_draw(rng, dims, scale, reach, cuts=(), kind=jnp.bfloat16):
    values = jax.random.normal(rng, dims, jnp.float32) * scale
    if len(cuts) > 0:
        values = level_of(rng, dims, cuts, -0.22, 0.18) * values
    return jnp.clip(values, min=-reach, max=reach).astype(kind)


def setup_inputs(seed: int = 0) -> dict:
    key_list = jax.random.split(jax.random.key(seed), 7)
    features = bell_draw(key_list[0], (CH, HEIGHT, WIDTH), 1.0, 6.0, ((1, 8), (2, 4)))
    labels = plant(jax.random.randint(key_list[1], (HEIGHT, WIDTH), 0, CLASSES), jax.random.fold_in(key_list[1], 1), 0, CLASSES - 1).astype(jnp.int32)
    w_input = bell_draw(key_list[2], (MID, CH), CH ** -0.5, 0.21875)
    w_dilate4 = bell_draw(key_list[3], (MID, 9 * MID), (9 * MID) ** -0.5, 0.1875)
    w_dilate8 = bell_draw(key_list[4], (MID, 9 * MID), (9 * MID) ** -0.5, 0.1875)
    w_classes = bell_draw(key_list[5], (CLASSES, MID), MID ** -0.5, 0.5)
    return {"features": features, "labels": labels, "w_input": w_input, "w_dilate4": w_dilate4, "w_dilate8": w_dilate8, "w_classes": w_classes}


loss_weight = 0.03125

def smooth(value):
    return value * jax.nn.sigmoid(value)

def slope(value):
    sig = jax.nn.sigmoid(value)
    return sig * (1.0 + value * (1.0 - sig))

def shifted(field, down, right):
    height = field.shape[1]
    width = field.shape[2]
    padded = jnp.pad(field, ((0, 0), (8, 8), (8, 8)))
    return padded[:, 8 + down:8 + down + height, 8 + right:8 + right + width]

def convolve(field, weight, dilation, sign):
    chans = field.shape[0]
    total = jnp.zeros((weight.shape[0], field.shape[1] * field.shape[2]), jnp.float32)
    for tap in range(9):
        piece = shifted(field, sign * (tap // 3 - 1) * dilation, sign * (tap % 3 - 1) * dilation)
        total = total + jnp.dot(weight[:, tap * chans:(tap + 1) * chans], piece.reshape(chans, -1), preferred_element_type=jnp.float32)
    return total

def pixel_contract(left, right):
    return lax.dot_general(left, right, (((1,), (1,)), ((), ())), preferred_element_type=jnp.float32)

def kernel_grad(grad, field, dilation):
    chans = field.shape[0]
    blocks = []
    for tap in range(9):
        piece = shifted(field, (tap // 3 - 1) * dilation, (tap % 3 - 1) * dilation)
        blocks.append(pixel_contract(grad, piece.reshape(chans, -1)))
    return jnp.concatenate(blocks, 1)

def flipped(weight):
    chans = weight.shape[0]
    return weight.reshape(chans, 9, chans).transpose(2, 1, 0).reshape(chans, 9 * chans)

def reference(features, labels, w_input, w_dilate4, w_dilate8, w_classes):
    flat = features.reshape(CH, -1)
    a1 = jnp.dot(w_input, flat, preferred_element_type=jnp.float32)
    h1 = smooth(a1).astype(jnp.bfloat16).reshape(MID, HEIGHT, WIDTH)
    a2 = convolve(h1, w_dilate4, 4, 1)
    h2 = smooth(a2).astype(jnp.bfloat16).reshape(MID, HEIGHT, WIDTH)
    a3 = convolve(h2, w_dilate8, 8, 1)
    h3 = smooth(a3).astype(jnp.bfloat16)
    logits = jnp.dot(w_classes, h3, preferred_element_type=jnp.float32)
    expo = jnp.exp(logits)
    prob = expo / lax.optimization_barrier(jnp.sum(expo, axis=0, keepdims=True))
    onehot = (labels.reshape(1, -1) == jnp.arange(CLASSES, dtype=jnp.int32)[:, None]).astype(jnp.float32)
    g4 = (loss_weight * (prob - onehot)).astype(jnp.bfloat16)
    grad_classes = pixel_contract(g4, h3)
    back3 = lax.dot_general(w_classes, g4, (((0,), (0,)), ((), ())), preferred_element_type=jnp.float32)
    g3 = (back3 * slope(a3)).astype(jnp.bfloat16)
    grad_dilate8 = kernel_grad(g3, h2, 8)
    back2 = convolve(g3.reshape(MID, HEIGHT, WIDTH), flipped(w_dilate8), 8, -1)
    g2 = (back2 * slope(a2)).astype(jnp.bfloat16)
    grad_dilate4 = kernel_grad(g2, h1, 4)
    back1 = convolve(g2.reshape(MID, HEIGHT, WIDTH), flipped(w_dilate4), 4, -1)
    g1 = (back1 * slope(a1)).astype(jnp.bfloat16)
    grad_input = pixel_contract(g1, flat)
    return (grad_input, grad_dilate4, grad_dilate8, grad_classes)
```

```python
import functools

import jax
import jax.numpy as jnp
from jax import lax
from jax.experimental import pallas as pl
from jax.experimental.pallas import tpu as pltpu
from jax.sharding import PartitionSpec as P

loss_weight = 0.03125
MESH = pl.DeviceIdType.MESH
BF = jnp.bfloat16
F32 = jnp.float32
HALO = 12
SIDE = 16


def nn(a, b):
    return lax.dot_general(a, b, (((1,), (0,)), ((), ())), preferred_element_type=F32)


def nt(a, b):
    return lax.dot_general(a, b, (((1,), (1,)), ((), ())), preferred_element_type=F32)


def tn(a, b):
    return lax.dot_general(a, b, (((0,), (0,)), ((), ())), preferred_element_type=F32)


def act(a):
    sig = 1.0 / (1.0 + jnp.exp(-a))
    return a * sig, sig * (1.0 + a * (1.0 - sig))


def flat2(v):
    return v.reshape(v.shape[0] * v.shape[1], v.shape[2])


class Halo:
    def __init__(self, buf, send, recv, me, counts, rows, cols):
        self.items = []
        (r, c), (nr, nc) = me, counts
        index = 0
        for dr in (-1, 1, 0):
            for dc in (0, -1, 1):
                if dr == 0 and dc == 0:
                    continue
                sr, dst_r, n_r = {
                    -1: (HALO, HALO + rows, HALO),
                    0: (HALO, HALO, rows),
                    1: (rows, 0, HALO),
                }[dr]
                sc, dst_c, n_c = {
                    -1: (SIDE, SIDE + cols, SIDE),
                    0: (SIDE, SIDE, cols),
                    1: (cols, 0, SIDE),
                }[dc]
                to_ok = self.inside(r + dr, nr) & self.inside(c + dc, nc)
                from_ok = self.inside(r - dr, nr) & self.inside(c - dc, nc)
                copy = functools.partial(
                    pltpu.make_async_remote_copy,
                    src_ref=buf.at[pl.ds(sr, n_r), pl.ds(sc, n_c), :],
                    dst_ref=buf.at[pl.ds(dst_r, n_r), pl.ds(dst_c, n_c), :],
                    send_sem=send.at[index],
                    recv_sem=recv.at[index],
                    device_id=(r + dr, c + dc),
                    device_id_type=MESH,
                )
                self.items.append((copy, to_ok, from_ok))
                index += 1

    @staticmethod
    def inside(i, n):
        return (i >= 0) & (i < n)

    def start(self):
        for copy, to_ok, _ in self.items:
            pl.when(to_ok)(lambda copy=copy: copy().start())

    def wait_recv(self):
        for copy, _, from_ok in self.items:
            pl.when(from_ok)(lambda copy=copy: copy().wait_recv())

    def wait_send(self):
        for copy, to_ok, _ in self.items:
            pl.when(to_ok)(lambda copy=copy: copy().wait_send())


class Reduce:
    def __init__(self, bufs, me, counts):
        self.snd, self.rc1, self.s2, self.rc2, self.ag, self.send, self.recv = bufs
        self.me, self.counts = me, counts
        total = self.snd.shape[0]
        self.blk = total // counts[1]
        self.piece = self.blk // counts[0]
        self.sem = 0
        self.copies = []

    def push(self, src, dst, device):
        copy = pltpu.make_async_remote_copy(
            src_ref=src,
            dst_ref=dst,
            send_sem=self.send.at[self.sem],
            recv_sem=self.recv.at[self.sem],
            device_id=device,
            device_id_type=MESH,
        )
        self.sem += 1
        copy.start()
        self.copies.append(copy)
        return copy

    def at(self, index, size):
        return pl.ds(pl.multiple_of(index * size, 16), size)

    def phase1(self):
        (r, c), (_, nc) = self.me, self.counts
        self.now = [
            self.push(
                self.snd.at[self.at(lax.rem(c + k, nc), self.blk), :],
                self.rc1.at[k - 1],
                (r, lax.rem(c + k, nc)),
            )
            for k in range(1, nc)
        ]

    def phase2(self):
        (r, c), (nr, nc) = self.me, self.counts
        acc = self.snd[self.at(c, self.blk), :].astype(F32)
        for k, copy in enumerate(self.now):
            copy.wait_recv()
            acc = acc + self.rc1[k].astype(F32)
        self.s2[...] = acc.astype(BF)
        self.now = [
            self.push(
                self.s2.at[self.at(lax.rem(r + k, nr), self.piece), :],
                self.rc2.at[k - 1],
                (lax.rem(r + k, nr), c),
            )
            for k in range(1, nr)
        ]

    def phase3(self):
        (r, c), (nr, nc) = self.me, self.counts
        acc = self.s2[self.at(r, self.piece), :].astype(F32)
        for k, copy in enumerate(self.now):
            copy.wait_recv()
            acc = acc + self.rc2[k].astype(F32)
        spot = self.at(c * nr + r, self.piece)
        self.ag[spot, :] = acc.astype(BF)
        self.now = [
            self.push(self.ag.at[spot, :], self.ag.at[spot, :], (lax.rem(r + k, nr), c))
            for k in range(1, nr)
        ]

    def phase4(self):
        (r, c), (_, nc) = self.me, self.counts
        for copy in self.now:
            copy.wait_recv()
        spot = self.at(c, self.blk)
        self.now = [
            self.push(self.ag.at[spot, :], self.ag.at[spot, :], (r, lax.rem(c + k, nc)))
            for k in range(1, nc)
        ]

    def finish(self):
        for copy in self.now:
            copy.wait_recv()

    def drain(self):
        for copy in self.copies:
            copy.wait_send()


def kernel(counts, rows, cols, *refs):
    (flat_ref, lab_ref, wi_ref, w4_ref, w8_ref, wc_ref, oi_ref, o4_ref, o8_ref, oc_ref) = refs[:10]
    (w1, x4, s1, s2, h2, x8, s3, w3, xg, g2p, g2o, xg4, g1, wt4, wt8) = refs[10:25]
    hs1, hr1, hs2, hr2 = refs[25:29]
    bufs_a, bufs_b = refs[29:36], refs[36:43]
    nr, nc = counts
    me = (lax.axis_index("rows"), lax.axis_index("cols"))
    r, c = me
    mid = wi_ref.shape[0]
    chans = wi_ref.shape[1]
    classes = wc_ref.shape[0]
    wide = cols + 16

    w1[...] = jnp.zeros_like(w1)
    w3[...] = jnp.zeros_like(w3)
    barrier = pltpu.get_barrier_semaphore()
    partners = [(lax.rem(r + k, nr), c) for k in range(1, nr)]
    partners += [(r, lax.rem(c + k, nc)) for k in range(1, nc)]
    partners += [(lax.rem(r + dr, nr), lax.rem(c + dc, nc)) for dr in (1, nr - 1) for dc in (1, nc - 1)]
    for device in partners:
        pl.semaphore_signal(barrier, inc=1, device_id=device, device_id_type=MESH)

    for t in range(9):
        wt4[(8 - t) * mid : (9 - t) * mid, :] = w4_ref[:, t * mid : (t + 1) * mid]
        wt8[(8 - t) * mid : (9 - t) * mid, :] = w8_ref[:, t * mid : (t + 1) * mid]

    def first(y, _):
        part = flat_ref[:, pl.ds(pl.multiple_of(y * 4 * cols, 128), 4 * cols)]
        a1 = nn(wi_ref[...], part).T
        h, s = act(a1)
        w1[pl.ds(HALO + 4 * y, 4), SIDE : SIDE + cols, :] = h.astype(BF).reshape(4, cols, mid)
        s1[pl.ds(4 * y, 4)] = s.reshape(4, cols, mid)
        return 0

    lax.fori_loop(0, rows // 4, first, 0)

    pl.semaphore_wait(barrier, len(partners))

    halo1 = Halo(w1, hs1, hr1, me, counts, rows, cols)
    halo1.start()
    halo1.wait_recv()

    def shift_into(dst, src, starts, width):
        for k, start in enumerate(starts):
            piece = src[:, start : start + width, :]
            dst[:, :, k * mid : (k + 1) * mid] = piece

    shift_into(x4, w1, (4, 8, 12), wide)

    def taps(x, base, step, count):
        return flat2(
            jnp.concatenate([x[pl.ds(base + step * k, count)] for k in range(3)], axis=-1)
        )

    def mask(row0, count):
        rp = r * rows + row0 + lax.broadcasted_iota(jnp.int32, (count, wide, mid), 0)
        cp = c * cols - 8 + lax.broadcasted_iota(jnp.int32, (count, wide, mid), 1)
        ok = (rp >= 0) & (rp < rows * nr) & (cp >= 0) & (cp < cols * nc)
        return ok.astype(F32)

    def second(b, _):
        a2 = nt(taps(x4, 8 * b, 4, 8), w4_ref[...])
        h, s = act(a2)
        m = mask(8 * b - 8, 8)
        h2[pl.ds(8 * b, 8)] = (h.reshape(8, wide, mid) * m).astype(BF)
        s2[pl.ds(8 * b, 8)] = s.reshape(8, wide, mid) * m
        return 0

    lax.fori_loop(0, (rows + 16) // 8, second, 0)
    shift_into(x8, h2, (0, 8, 16), cols)

    red_a = Reduce(bufs_a, me, counts)
    red_b = Reduce(bufs_b, me, counts)

    gc = jnp.zeros((classes, mid), F32)
    for b in range(rows // 8):
        a3 = nt(taps(x8, 8 * b, 8, 8), w8_ref[...])
        h3, s3v = act(a3)
        h3 = h3.astype(BF)
        expo = jnp.exp(nt(wc_ref[...], h3))
        prob = expo / jnp.sum(expo, axis=0, keepdims=True)
        label = jnp.concatenate(
            [
                jnp.broadcast_to(lab_ref[8 * b + j : 8 * b + j + 1, :], (classes, cols))
                for j in range(8)
            ],
            axis=1,
        )
        onehot = (label == lax.broadcasted_iota(jnp.int32, label.shape, 0)).astype(F32)
        g4 = (loss_weight * (prob - onehot)).astype(BF)
        gc = gc + nn(g4, h3)
        g3 = (tn(g4, wc_ref[...]) * s3v).astype(BF)
        w3[HALO + 8 * b : HALO + 8 * b + 8, SIDE : SIDE + cols, :] = g3.reshape(8, cols, mid)

    halo2 = Halo(w3, hs2, hr2, me, counts, rows, cols)
    halo2.start()

    def zero_tail(red, used):
        total = red.snd.shape[0]
        if total > used:
            red.snd[used:, :] = jnp.zeros((total - used, mid), BF)

    g3_t = flat2(w3[HALO : HALO + rows, SIDE : SIDE + cols, :]).T
    for ky in range(3):
        block = nn(g3_t, flat2(x8[8 * ky : 8 * ky + rows]))
        for kx in range(3):
            t = 3 * ky + kx
            red_a.snd[t * mid : (t + 1) * mid, :] = block[:, kx * mid : (kx + 1) * mid].astype(BF)
    red_a.snd[9 * mid : 9 * mid + classes, :] = gc.astype(BF)
    zero_tail(red_a, 9 * mid + classes)
    red_a.phase1()

    halo2.wait_recv()
    shift_into(xg, w3, (0, 8, 16), wide)

    def third(b, _):
        back = nn(taps(xg, 8 * b, 8, 8), wt8[...])
        g2p[pl.ds(8 * b, 8)] = (back.reshape(8, wide, mid) * s2[pl.ds(8 * b + 4, 8)]).astype(BF)
        return 0

    lax.fori_loop(0, (rows + 8) // 8, third, 0)
    red_a.phase2()

    shift_into(xg4, g2p, (4, 8, 12), cols)
    spot = lax.broadcasted_iota(jnp.int32, (rows, wide, mid), 1)
    own = (spot >= 8) & (spot < 8 + cols)
    g2o[...] = jnp.where(own, g2p[4 : 4 + rows].astype(F32), 0.0).astype(BF)

    g2_t = flat2(g2o[...]).T
    for ky in range(3):
        block = nn(g2_t, flat2(x4[8 + 4 * ky : 8 + 4 * ky + rows]))
        for kx in range(3):
            t = 3 * ky + kx
            red_b.snd[t * mid : (t + 1) * mid, :] = block[:, kx * mid : (kx + 1) * mid].astype(BF)
    red_a.phase3()

    def fourth(b, _):
        back = nn(taps(xg4, 8 * b, 4, 8), wt4[...])
        s = flat2(s1[pl.ds(8 * b, 8)])
        g1[pl.ds(pl.multiple_of(b * 8 * cols, 128), 8 * cols), :] = (back * s).astype(BF)
        return 0

    lax.fori_loop(0, rows // 8, fourth, 0)
    base = 9 * mid
    gi = nn(flat_ref[...], g1[...])
    for k in range(chans // mid):
        block = gi[k * mid : (k + 1) * mid, :].T
        red_b.snd[base + k * mid : base + (k + 1) * mid, :] = block.astype(BF)
    zero_tail(red_b, base + chans)
    red_b.phase1()
    red_a.phase4()
    red_b.phase2()
    red_a.finish()
    for t in range(9):
        o8_ref[:, t * mid : (t + 1) * mid] = red_a.ag[t * mid : (t + 1) * mid, :].astype(F32)
    oc_ref[...] = red_a.ag[9 * mid : 9 * mid + classes, :].astype(F32)
    red_b.phase3()
    red_b.phase4()
    red_b.finish()
    for t in range(9):
        o4_ref[:, t * mid : (t + 1) * mid] = red_b.ag[t * mid : (t + 1) * mid, :].astype(F32)
    for k in range(chans // mid):
        lo = base + k * mid
        oi_ref[:, k * mid : (k + 1) * mid] = red_b.ag[lo : lo + mid, :].astype(F32)
    halo1.wait_send()
    halo2.wait_send()
    red_a.drain()
    red_b.drain()


def reduce_scratch(used, counts):
    nr, nc = counts
    unit = 16 * nr * nc
    total = -(-used // unit) * unit
    blk = total // nc
    piece = blk // nr
    sems = 2 * (nr - 1) + 2 * (nc - 1)
    return [
        pltpu.VMEM((total, 128), BF),
        pltpu.VMEM((max(nc - 1, 1), blk, 128), BF),
        pltpu.VMEM((blk, 128), BF),
        pltpu.VMEM((max(nr - 1, 1), piece, 128), BF),
        pltpu.VMEM((total, 128), BF),
        pltpu.SemaphoreType.DMA((sems,)),
        pltpu.SemaphoreType.DMA((sems,)),
    ]


def local(counts, features, labels, w_input, w_dilate4, w_dilate8, w_classes):
    chans, rows, cols = features.shape
    mid = w_input.shape[0]
    classes = w_classes.shape[0]
    wide = cols + 16
    flat = features.reshape(chans, rows * cols)
    vmem = pl.BlockSpec(memory_space=pltpu.VMEM)
    scratch = [
        pltpu.VMEM((rows + 24, cols + 32, mid), BF),
        pltpu.VMEM((rows + 24, wide, 3 * mid), BF),
        pltpu.VMEM((rows, cols, mid), F32),
        pltpu.VMEM((rows + 16, wide, mid), F32),
        pltpu.VMEM((rows + 16, wide, mid), BF),
        pltpu.VMEM((rows + 16, cols, 3 * mid), BF),
        pltpu.VMEM((8, 128), F32),
        pltpu.VMEM((rows + 24, cols + 32, mid), BF),
        pltpu.VMEM((rows + 24, wide, 3 * mid), BF),
        pltpu.VMEM((rows + 8, wide, mid), BF),
        pltpu.VMEM((rows, wide, mid), BF),
        pltpu.VMEM((rows + 8, cols, 3 * mid), BF),
        pltpu.VMEM((rows * cols, mid), BF),
        pltpu.VMEM((9 * mid, mid), BF),
        pltpu.VMEM((9 * mid, mid), BF),
    ]
    scratch += [pltpu.SemaphoreType.DMA((8,))] * 4
    scratch += reduce_scratch(9 * mid + classes, counts)
    scratch += reduce_scratch(9 * mid + chans, counts)
    return pl.pallas_call(
        functools.partial(kernel, counts, rows, cols),
        out_shape=(
            jax.ShapeDtypeStruct((mid, chans), F32),
            jax.ShapeDtypeStruct((mid, 9 * mid), F32),
            jax.ShapeDtypeStruct((mid, 9 * mid), F32),
            jax.ShapeDtypeStruct((classes, mid), F32),
        ),
        in_specs=[vmem] * 6,
        out_specs=(vmem,) * 4,
        scratch_shapes=scratch,
        compiler_params=pltpu.CompilerParams(
            collective_id=0, has_side_effects=True, vmem_limit_bytes=56 * 1024 * 1024
        ),
        cost_estimate=pl.CostEstimate(
            flops=6_000_000_000, bytes_accessed=8_000_000, transcendentals=1_000_000
        ),
    )(flat, labels, w_input, w_dilate4, w_dilate8, w_classes)


def solution(mesh):
    counts = (mesh.shape["rows"], mesh.shape["cols"])
    return jax.shard_map(
        functools.partial(local, counts),
        mesh=mesh,
        in_specs=(P(None, "rows", "cols"), P("rows", "cols"), P(), P(), P(), P()),
        out_specs=(P(), P(), P(), P()),
        check_vma=False,
    )
```

```python
import functools

import jax
import jax.numpy as jnp
from jax import lax
from jax.experimental import pallas as pl
from jax.experimental.pallas import tpu as pltpu
from jax.sharding import PartitionSpec as P

loss_weight = 0.03125
MESH = pl.DeviceIdType.MESH
BF = jnp.bfloat16
F32 = jnp.float32
HALO = 12
SIDE = 16


def nn(a, b):
    return lax.dot_general(a, b, (((1,), (0,)), ((), ())), preferred_element_type=F32)


def nt(a, b):
    return lax.dot_general(a, b, (((1,), (1,)), ((), ())), preferred_element_type=F32)


def tn(a, b):
    return lax.dot_general(a, b, (((0,), (0,)), ((), ())), preferred_element_type=F32)


def act(a):
    sig = 0.5 * jnp.tanh(0.5 * a) + 0.5
    return a * sig, sig * (1.0 + a * (1.0 - sig))


def inside(i, n):
    return (i >= 0) & (i < n)


def flat2(v):
    return v.reshape(v.shape[0] * v.shape[1], v.shape[2])


class Halo:
    def __init__(self, buf, send, recv, me, counts, rows, cols, skip, depth):
        self.items = []
        (r, c), (nr, nc) = me, counts
        index = 0
        for dr in (-1, 1, 0):
            for dc in (0, -1, 1):
                if dr == 0 and (dc == 0 or skip > 0):
                    continue
                sr, dst_r, n_r = {
                    -1: (HALO + skip, HALO + rows + skip, depth),
                    0: (HALO, HALO, rows),
                    1: (HALO + rows - skip - depth, HALO - skip - depth, depth),
                }[dr]
                sc, dst_c, n_c = {
                    -1: (SIDE, SIDE + cols, SIDE),
                    0: (SIDE, SIDE, cols),
                    1: (cols, 0, SIDE),
                }[dc]
                to_ok = inside(r + dr, nr) & inside(c + dc, nc)
                from_ok = inside(r - dr, nr) & inside(c - dc, nc)
                copy = functools.partial(
                    pltpu.make_async_remote_copy,
                    src_ref=buf.at[pl.ds(sr, n_r), pl.ds(sc, n_c), :],
                    dst_ref=buf.at[pl.ds(dst_r, n_r), pl.ds(dst_c, n_c), :],
                    send_sem=send.at[index],
                    recv_sem=recv.at[index],
                    device_id=(r + dr, c + dc),
                    device_id_type=MESH,
                )
                self.items.append((copy, to_ok, from_ok))
                index += 1

    def start(self):
        for copy, to_ok, _ in self.items:
            pl.when(to_ok)(lambda copy=copy: copy().start())

    def wait_recv(self):
        for copy, _, from_ok in self.items:
            pl.when(from_ok)(lambda copy=copy: copy().wait_recv())

    def wait_send(self):
        for copy, to_ok, _ in self.items:
            pl.when(to_ok)(lambda copy=copy: copy().wait_send())


class Reduce:
    def __init__(self, bufs, me, counts):
        self.snd, self.rc1, self.s2, self.rc2, self.ag, self.send, self.recv = bufs
        self.me, self.counts = me, counts
        total = self.snd.shape[0]
        self.blk = total // counts[1]
        self.piece = self.blk // counts[0]
        self.sem = 0
        self.copies = []

    def push(self, src, dst, device):
        copy = pltpu.make_async_remote_copy(
            src_ref=src,
            dst_ref=dst,
            send_sem=self.send.at[self.sem],
            recv_sem=self.recv.at[self.sem],
            device_id=device,
            device_id_type=MESH,
        )
        self.sem += 1
        copy.start()
        self.copies.append(copy)
        return copy

    def at(self, index, size):
        return pl.ds(pl.multiple_of(index * size, 16), size)

    def phase1(self):
        (r, c), (_, nc) = self.me, self.counts
        self.now = [
            self.push(
                self.snd.at[self.at(lax.rem(c + k, nc), self.blk), :],
                self.rc1.at[k - 1],
                (r, lax.rem(c + k, nc)),
            )
            for k in range(1, nc)
        ]

    def phase2(self):
        (r, c), (nr, nc) = self.me, self.counts
        acc = self.snd[self.at(c, self.blk), :].astype(F32)
        for k, copy in enumerate(self.now):
            copy.wait_recv()
            acc = acc + self.rc1[k].astype(F32)
        self.s2[...] = acc.astype(BF)
        self.now = [
            self.push(
                self.s2.at[self.at(lax.rem(r + k, nr), self.piece), :],
                self.rc2.at[k - 1],
                (lax.rem(r + k, nr), c),
            )
            for k in range(1, nr)
        ]

    def phase3(self):
        (r, c), (nr, nc) = self.me, self.counts
        acc = self.s2[self.at(r, self.piece), :].astype(F32)
        for k, copy in enumerate(self.now):
            copy.wait_recv()
            acc = acc + self.rc2[k].astype(F32)
        spot = self.at(c * nr + r, self.piece)
        self.ag[spot, :] = acc.astype(BF)
        self.now = [
            self.push(self.ag.at[spot, :], self.ag.at[spot, :], (lax.rem(r + k, nr), c))
            for k in range(1, nr)
        ]

    def phase4(self):
        (r, c), (_, nc) = self.me, self.counts
        for copy in self.now:
            copy.wait_recv()
        spot = self.at(c, self.blk)
        self.now = [
            self.push(self.ag.at[spot, :], self.ag.at[spot, :], (r, lax.rem(c + k, nc)))
            for k in range(1, nc)
        ]

    def finish(self):
        for copy in self.now:
            copy.wait_recv()

    def drain(self):
        for copy in self.copies:
            copy.wait_send()


def kernel(counts, rows, cols, *refs):
    (flat_ref, lab_ref, wi_ref, w4_ref, w8_ref, wc_ref, oi_ref, o4_ref, o8_ref, oc_ref) = refs[:10]
    (w1, x4, s1, s2, h2, x8, w3, xg, g2p, g2o, xg4, g1, wt4, wt8) = refs[10:24]
    halo_sems = refs[24:32]
    bufs_a, bufs_d, bufs_i = refs[32:39], refs[39:46], refs[46:53]
    nr, nc = counts
    me = (lax.axis_index("rows"), lax.axis_index("cols"))
    r, c = me
    mid = wi_ref.shape[0]
    chans = wi_ref.shape[1]
    classes = wc_ref.shape[0]
    wide = cols + 16

    w1[...] = jnp.zeros_like(w1)
    w3[...] = jnp.zeros_like(w3)
    barrier = pltpu.get_barrier_semaphore()
    partners = [(lax.rem(r + k, nr), c) for k in range(1, nr)]
    partners += [(r, lax.rem(c + k, nc)) for k in range(1, nc)]
    partners += [(lax.rem(r + dr, nr), lax.rem(c + dc, nc)) for dr in (1, nr - 1) for dc in (1, nc - 1)]
    for device in partners:
        pl.semaphore_signal(barrier, inc=1, device_id=device, device_id_type=MESH)

    for t in range(9):
        wt4[(8 - t) * mid : (9 - t) * mid, :] = w4_ref[:, t * mid : (t + 1) * mid]
        wt8[(8 - t) * mid : (9 - t) * mid, :] = w8_ref[:, t * mid : (t + 1) * mid]

    def first(y, _):
        part = flat_ref[:, pl.ds(pl.multiple_of(y * 4 * cols, 128), 4 * cols)]
        a1 = nn(wi_ref[...], part).T
        h, s = act(a1)
        w1[pl.ds(HALO + 4 * y, 4), SIDE : SIDE + cols, :] = h.astype(BF).reshape(4, cols, mid)
        s1[pl.ds(4 * y, 4)] = s.reshape(4, cols, mid)
        return 0

    lax.fori_loop(0, rows // 4, first, 0)

    pl.semaphore_wait(barrier, len(partners))

    def halo(buf, slot, skip, depth):
        send, recv = halo_sems[2 * slot : 2 * slot + 2]
        return Halo(buf, send, recv, me, counts, rows, cols, skip, depth)

    near1, far1 = halo(w1, 0, 0, 4), halo(w1, 1, 4, HALO - 4)
    near1.start()
    far1.start()

    def shift_into(dst, src, starts, width, lo, hi):
        for k, start in enumerate(starts):
            piece = src[lo:hi, start : start + width, :]
            dst[lo:hi, :, k * mid : (k + 1) * mid] = piece

    def taps(x, base, step, count):
        return flat2(
            jnp.concatenate([x[pl.ds(base + step * k, count)] for k in range(3)], axis=-1)
        )

    def mask(row0, count):
        rp = r * rows + row0 + lax.broadcasted_iota(jnp.int32, (count, wide, mid), 0)
        cp = c * cols - 8 + lax.broadcasted_iota(jnp.int32, (count, wide, mid), 1)
        ok = (rp >= 0) & (rp < rows * nr) & (cp >= 0) & (cp < cols * nc)
        return ok.astype(F32)

    def second(b, _):
        a2 = nt(taps(x4, 8 * b, 4, 8), w4_ref[...])
        h, s = act(a2)
        m = mask(8 * b - 8, 8)
        h2[pl.ds(8 * b, 8)] = (h.reshape(8, wide, mid) * m).astype(BF)
        s2[pl.ds(8 * b, 8)] = s.reshape(8, wide, mid) * m
        return 0

    near1.wait_recv()
    shift_into(x4, w1, (4, 8, 12), wide, 8, rows + 16)
    lax.fori_loop(1, rows // 8 + 1, second, 0)
    shift_into(x8, h2, (0, 8, 16), cols, 8, rows + 8)
    far1.wait_recv()
    for lo, hi in ((0, 8), (rows + 16, rows + 24)):
        shift_into(x4, w1, (4, 8, 12), wide, lo, hi)
    for b, lo in ((0, 0), (rows // 8 + 1, rows + 8)):
        second(b, 0)
        shift_into(x8, h2, (0, 8, 16), cols, lo, lo + 8)

    red_a = Reduce(bufs_a, me, counts)
    red_d = Reduce(bufs_d, me, counts)
    red_i = Reduce(bufs_i, me, counts)

    gc = jnp.zeros((classes, mid), F32)
    for b in range(rows // 8):
        a3 = nt(taps(x8, 8 * b, 8, 8), w8_ref[...])
        h3, s3v = act(a3)
        h3 = h3.astype(BF)
        expo = jnp.exp(nt(wc_ref[...], h3))
        prob = expo / jnp.sum(expo, axis=0, keepdims=True)
        label = jnp.concatenate(
            [
                jnp.broadcast_to(lab_ref[8 * b + j : 8 * b + j + 1, :], (classes, cols))
                for j in range(8)
            ],
            axis=1,
        )
        onehot = (label == lax.broadcasted_iota(jnp.int32, label.shape, 0)).astype(F32)
        g4 = (loss_weight * (prob - onehot)).astype(BF)
        gc = gc + nn(g4, h3)
        g3 = (tn(g4, wc_ref[...]) * s3v).astype(BF)
        w3[HALO + 8 * b : HALO + 8 * b + 8, SIDE : SIDE + cols, :] = g3.reshape(8, cols, mid)

    near2, far2 = halo(w3, 2, 0, 8), halo(w3, 3, 8, HALO - 8)
    near2.start()
    far2.start()

    def zero_tail(red, used):
        total = red.snd.shape[0]
        if total > used:
            red.snd[used:, :] = jnp.zeros((total - used, mid), BF)

    g3_t = flat2(w3[HALO : HALO + rows, SIDE : SIDE + cols, :]).T
    for ky in range(3):
        block = nn(g3_t, flat2(x8[8 * ky : 8 * ky + rows]))
        for kx in range(3):
            t = 3 * ky + kx
            red_a.snd[t * mid : (t + 1) * mid, :] = block[:, kx * mid : (kx + 1) * mid].astype(BF)
    red_a.snd[9 * mid : 9 * mid + classes, :] = gc.astype(BF)
    zero_tail(red_a, 9 * mid + classes)
    red_a.phase1()

    def third(base, count):
        back = nn(taps(xg, base, 8, count), wt8[...])
        grad = back.reshape(count, wide, mid) * s2[pl.ds(base + 4, count)]
        g2p[pl.ds(base, count)] = grad.astype(BF)

    near2.wait_recv()
    shift_into(xg, w3, (0, 8, 16), wide, 4, rows + 20)

    def third_own(b, _):
        third(8 * b + 4, 8)
        return 0

    lax.fori_loop(0, rows // 8, third_own, 0)
    red_a.phase2()

    spot = lax.broadcasted_iota(jnp.int32, (rows, wide, mid), 1)
    own = (spot >= 8) & (spot < 8 + cols)
    g2o[...] = jnp.where(own, g2p[4 : 4 + rows].astype(F32), 0.0).astype(BF)
    g2_t = flat2(g2o[...]).T
    for ky in range(3):
        block = nn(g2_t, flat2(x4[8 + 4 * ky : 8 + 4 * ky + rows]))
        for kx in range(3):
            t = 3 * ky + kx
            red_d.snd[t * mid : (t + 1) * mid, :] = block[:, kx * mid : (kx + 1) * mid].astype(BF)
    zero_tail(red_d, 9 * mid)
    red_d.phase1()
    red_a.phase3()
    shift_into(xg4, g2p, (4, 8, 12), cols, 4, rows + 4)

    far2.wait_recv()
    for lo in (0, rows + 20):
        shift_into(xg, w3, (0, 8, 16), wide, lo, lo + 4)
    for lo in (0, rows + 4):
        third(lo, 4)
        shift_into(xg4, g2p, (4, 8, 12), cols, lo, lo + 4)

    def fourth(b, _):
        back = nn(taps(xg4, 8 * b, 4, 8), wt4[...])
        s = flat2(s1[pl.ds(8 * b, 8)])
        g1[pl.ds(pl.multiple_of(b * 8 * cols, 128), 8 * cols), :] = (back * s).astype(BF)
        return 0

    lax.fori_loop(0, rows // 8, fourth, 0)
    red_d.phase2()
    gi = nn(flat_ref[...], g1[...])
    for k in range(chans // mid):
        block = gi[k * mid : (k + 1) * mid, :].T
        red_i.snd[k * mid : (k + 1) * mid, :] = block.astype(BF)
    zero_tail(red_i, chans)
    red_i.phase1()
    red_a.phase4()
    red_d.phase3()
    red_i.phase2()
    red_d.phase4()
    red_i.phase3()
    red_a.finish()
    for t in range(9):
        o8_ref[:, t * mid : (t + 1) * mid] = red_a.ag[t * mid : (t + 1) * mid, :]
    oc_ref[...] = red_a.ag[9 * mid : 9 * mid + classes, :]
    red_i.phase4()
    red_d.finish()
    for t in range(9):
        o4_ref[:, t * mid : (t + 1) * mid] = red_d.ag[t * mid : (t + 1) * mid, :]
    red_i.finish()
    for k in range(chans // mid):
        oi_ref[:, k * mid : (k + 1) * mid] = red_i.ag[k * mid : (k + 1) * mid, :]
    for item in (near1, far1, near2, far2):
        item.wait_send()
    for red in (red_a, red_d, red_i):
        red.drain()


def reduce_scratch(used, counts):
    nr, nc = counts
    unit = 16 * nr * nc
    total = -(-used // unit) * unit
    blk = total // nc
    piece = blk // nr
    sems = 2 * (nr - 1) + 2 * (nc - 1)
    return [
        pltpu.VMEM((total, 128), BF),
        pltpu.VMEM((max(nc - 1, 1), blk, 128), BF),
        pltpu.VMEM((blk, 128), BF),
        pltpu.VMEM((max(nr - 1, 1), piece, 128), BF),
        pltpu.VMEM((total, 128), BF),
        pltpu.SemaphoreType.DMA((sems,)),
        pltpu.SemaphoreType.DMA((sems,)),
    ]


def local(counts, features, labels, w_input, w_dilate4, w_dilate8, w_classes):
    chans, rows, cols = features.shape
    mid = w_input.shape[0]
    classes = w_classes.shape[0]
    wide = cols + 16
    flat = features.reshape(chans, rows * cols)
    vmem = pl.BlockSpec(memory_space=pltpu.VMEM)
    scratch = [
        pltpu.VMEM((rows + 24, cols + 32, mid), BF),
        pltpu.VMEM((rows + 24, wide, 3 * mid), BF),
        pltpu.VMEM((rows, cols, mid), F32),
        pltpu.VMEM((rows + 16, wide, mid), F32),
        pltpu.VMEM((rows + 16, wide, mid), BF),
        pltpu.VMEM((rows + 16, cols, 3 * mid), BF),
        pltpu.VMEM((rows + 24, cols + 32, mid), BF),
        pltpu.VMEM((rows + 24, wide, 3 * mid), BF),
        pltpu.VMEM((rows + 8, wide, mid), BF),
        pltpu.VMEM((rows, wide, mid), BF),
        pltpu.VMEM((rows + 8, cols, 3 * mid), BF),
        pltpu.VMEM((rows * cols, mid), BF),
        pltpu.VMEM((9 * mid, mid), BF),
        pltpu.VMEM((9 * mid, mid), BF),
    ]
    scratch += [pltpu.SemaphoreType.DMA((8,))] * 8
    scratch += reduce_scratch(9 * mid + classes, counts)
    scratch += reduce_scratch(9 * mid, counts)
    scratch += reduce_scratch(chans, counts)
    grads = pl.pallas_call(
        functools.partial(kernel, counts, rows, cols),
        out_shape=(
            jax.ShapeDtypeStruct((mid, chans), BF),
            jax.ShapeDtypeStruct((mid, 9 * mid), BF),
            jax.ShapeDtypeStruct((mid, 9 * mid), BF),
            jax.ShapeDtypeStruct((classes, mid), BF),
        ),
        in_specs=[vmem] * 6,
        out_specs=(vmem,) * 4,
        scratch_shapes=scratch,
        compiler_params=pltpu.CompilerParams(
            collective_id=0, has_side_effects=True, vmem_limit_bytes=56 * 1024 * 1024
        ),
        cost_estimate=pl.CostEstimate(
            flops=6_000_000_000, bytes_accessed=8_000_000, transcendentals=1_000_000
        ),
    )(flat, labels, w_input, w_dilate4, w_dilate8, w_classes)
    return tuple(grad.astype(F32) for grad in grads)


def solution(mesh):
    counts = (mesh.shape["rows"], mesh.shape["cols"])
    return jax.shard_map(
        functools.partial(local, counts),
        mesh=mesh,
        in_specs=(P(None, "rows", "cols"), P("rows", "cols"), P(), P(), P(), P()),
        out_specs=(P(), P(), P(), P()),
        check_vma=False,
    )
```

```python
import functools

import jax
import jax.numpy as jnp
from jax import lax
from jax.experimental import pallas as pl
from jax.experimental.pallas import tpu as pltpu
from jax.sharding import PartitionSpec as P

loss_weight = 0.03125
MESH = pl.DeviceIdType.MESH
BF = jnp.bfloat16
F32 = jnp.float32
HALO = 12
SIDE = 16


def nn(a, b):
    return lax.dot_general(a, b, (((1,), (0,)), ((), ())), preferred_element_type=F32)


def nt(a, b):
    return lax.dot_general(a, b, (((1,), (1,)), ((), ())), preferred_element_type=F32)


def tn(a, b):
    return lax.dot_general(a, b, (((0,), (0,)), ((), ())), preferred_element_type=F32)


def act(a):
    sig = 0.5 * jnp.tanh(0.5 * a) + 0.5
    return a * sig, sig * (1.0 + a * (1.0 - sig))


def inside(i, n):
    return (i >= 0) & (i < n)


def flat2(v):
    return v.reshape(v.shape[0] * v.shape[1], v.shape[2])


class Halo:
    def __init__(self, buf, send, recv, me, counts, rows, cols, skip, depth):
        self.items = []
        (r, c), (nr, nc) = me, counts
        index = 0
        for dr in (-1, 1, 0):
            for dc in (0, -1, 1):
                if dr == 0 and (dc == 0 or skip > 0):
                    continue
                sr, dst_r, n_r = {
                    -1: (HALO + skip, HALO + rows + skip, depth),
                    0: (HALO, HALO, rows),
                    1: (HALO + rows - skip - depth, HALO - skip - depth, depth),
                }[dr]
                sc, dst_c, n_c = {
                    -1: (SIDE, SIDE + cols, SIDE),
                    0: (SIDE, SIDE, cols),
                    1: (cols, 0, SIDE),
                }[dc]
                to_ok = inside(r + dr, nr) & inside(c + dc, nc)
                from_ok = inside(r - dr, nr) & inside(c - dc, nc)
                copy = functools.partial(
                    pltpu.make_async_remote_copy,
                    src_ref=buf.at[pl.ds(sr, n_r), pl.ds(sc, n_c), :],
                    dst_ref=buf.at[pl.ds(dst_r, n_r), pl.ds(dst_c, n_c), :],
                    send_sem=send.at[index],
                    recv_sem=recv.at[index],
                    device_id=(r + dr, c + dc),
                    device_id_type=MESH,
                )
                self.items.append((copy, to_ok, from_ok))
                index += 1

    def start(self):
        for copy, to_ok, _ in self.items:
            pl.when(to_ok)(lambda copy=copy: copy().start())

    def wait_recv(self):
        for copy, _, from_ok in self.items:
            pl.when(from_ok)(lambda copy=copy: copy().wait_recv())

    def wait_send(self):
        for copy, to_ok, _ in self.items:
            pl.when(to_ok)(lambda copy=copy: copy().wait_send())


class Reduce:
    def __init__(self, bufs, me, counts):
        self.snd, self.rc1, self.s2, self.rc2, self.ag, self.send, self.recv = bufs
        self.me, self.counts = me, counts
        total = self.snd.shape[0]
        self.blk = total // counts[1]
        self.piece = self.blk // counts[0]
        self.sem = 0
        self.copies = []

    def push(self, src, dst, device):
        copy = pltpu.make_async_remote_copy(
            src_ref=src,
            dst_ref=dst,
            send_sem=self.send.at[self.sem],
            recv_sem=self.recv.at[self.sem],
            device_id=device,
            device_id_type=MESH,
        )
        self.sem += 1
        copy.start()
        self.copies.append(copy)
        return copy

    def at(self, index, size):
        return pl.ds(pl.multiple_of(index * size, 16), size)

    def phase1(self):
        (r, c), (_, nc) = self.me, self.counts
        self.now = [
            self.push(
                self.snd.at[self.at(lax.rem(c + k, nc), self.blk), :],
                self.rc1.at[k - 1],
                (r, lax.rem(c + k, nc)),
            )
            for k in range(1, nc)
        ]

    def phase2(self):
        (r, c), (nr, nc) = self.me, self.counts
        acc = self.snd[self.at(c, self.blk), :].astype(F32)
        for k, copy in enumerate(self.now):
            copy.wait_recv()
            acc = acc + self.rc1[k].astype(F32)
        self.s2[...] = acc.astype(BF)
        self.now = [
            self.push(
                self.s2.at[self.at(lax.rem(r + k, nr), self.piece), :],
                self.rc2.at[k - 1],
                (lax.rem(r + k, nr), c),
            )
            for k in range(1, nr)
        ]

    def phase3(self):
        (r, c), (nr, nc) = self.me, self.counts
        acc = self.s2[self.at(r, self.piece), :].astype(F32)
        for k, copy in enumerate(self.now):
            copy.wait_recv()
            acc = acc + self.rc2[k].astype(F32)
        spot = self.at(c * nr + r, self.piece)
        self.ag[spot, :] = acc.astype(BF)
        self.now = [
            self.push(self.ag.at[spot, :], self.ag.at[spot, :], (lax.rem(r + k, nr), c))
            for k in range(1, nr)
        ]

    def phase4(self):
        (r, c), (_, nc) = self.me, self.counts
        for copy in self.now:
            copy.wait_recv()
        spot = self.at(c, self.blk)
        self.now = [
            self.push(self.ag.at[spot, :], self.ag.at[spot, :], (r, lax.rem(c + k, nc)))
            for k in range(1, nc)
        ]

    def finish(self):
        for copy in self.now:
            copy.wait_recv()

    def drain(self):
        for copy in self.copies:
            copy.wait_send()


def kernel(counts, rows, cols, *refs):
    (flat_ref, lab_ref, wi_ref, w4_ref, w8_ref, wc_ref, oi_ref, o4_ref, o8_ref, oc_ref) = refs[:10]
    (w1, x4, s1, s2, h2, x8, w3, xg, g2p, g2o, xg4, g1, wt4, wt8) = refs[10:24]
    halo_sems = refs[24:32]
    bufs_a, bufs_d, bufs_i = refs[32:39], refs[39:46], refs[46:53]
    nr, nc = counts
    me = (lax.axis_index("rows"), lax.axis_index("cols"))
    r, c = me
    mid = wi_ref.shape[0]
    chans = wi_ref.shape[1]
    classes = wc_ref.shape[0]
    wide = cols + 16

    w1[...] = jnp.zeros_like(w1)
    w3[...] = jnp.zeros_like(w3)
    barrier = pltpu.get_barrier_semaphore()
    partners = [(lax.rem(r + k, nr), c) for k in range(1, nr)]
    partners += [(r, lax.rem(c + k, nc)) for k in range(1, nc)]
    partners += [(lax.rem(r + dr, nr), lax.rem(c + dc, nc)) for dr in (1, nr - 1) for dc in (1, nc - 1)]
    for device in partners:
        pl.semaphore_signal(barrier, inc=1, device_id=device, device_id_type=MESH)

    for t in range(9):
        wt4[(8 - t) * mid : (9 - t) * mid, :] = w4_ref[:, t * mid : (t + 1) * mid]
        wt8[(8 - t) * mid : (9 - t) * mid, :] = w8_ref[:, t * mid : (t + 1) * mid]

    def first(y, _):
        part = flat_ref[:, pl.ds(pl.multiple_of(y * 4 * cols, 128), 4 * cols)]
        a1 = nn(wi_ref[...], part).T
        h, s = act(a1)
        w1[pl.ds(HALO + 4 * y, 4), SIDE : SIDE + cols, :] = h.astype(BF).reshape(4, cols, mid)
        s1[pl.ds(4 * y, 4)] = s.reshape(4, cols, mid)
        return 0

    lax.fori_loop(0, rows // 4, first, 0, unroll=True)

    pl.semaphore_wait(barrier, len(partners))

    def halo(buf, slot, skip, depth):
        send, recv = halo_sems[2 * slot : 2 * slot + 2]
        return Halo(buf, send, recv, me, counts, rows, cols, skip, depth)

    near1, far1 = halo(w1, 0, 0, 4), halo(w1, 1, 4, HALO - 4)
    near1.start()
    far1.start()

    def shift_into(dst, src, starts, width, lo, hi):
        for k, start in enumerate(starts):
            piece = src[lo:hi, start : start + width, :]
            dst[lo:hi, :, k * mid : (k + 1) * mid] = piece

    def taps(x, base, step, count):
        return flat2(
            jnp.concatenate([x[pl.ds(base + step * k, count)] for k in range(3)], axis=-1)
        )

    def mask(row0, count):
        rp = r * rows + row0 + lax.broadcasted_iota(jnp.int32, (count, wide, mid), 0)
        cp = c * cols - 8 + lax.broadcasted_iota(jnp.int32, (count, wide, mid), 1)
        ok = (rp >= 0) & (rp < rows * nr) & (cp >= 0) & (cp < cols * nc)
        return ok.astype(F32)

    def second(b, _):
        a2 = nt(taps(x4, 8 * b, 4, 8), w4_ref[...])
        h, s = act(a2)
        m = mask(8 * b - 8, 8)
        h2[pl.ds(8 * b, 8)] = (h.reshape(8, wide, mid) * m).astype(BF)
        s2[pl.ds(8 * b, 8)] = s.reshape(8, wide, mid) * m
        return 0

    near1.wait_recv()
    shift_into(x4, w1, (4, 8, 12), wide, 8, rows + 16)
    lax.fori_loop(1, rows // 8 + 1, second, 0, unroll=True)
    shift_into(x8, h2, (0, 8, 16), cols, 8, rows + 8)
    far1.wait_recv()
    for lo, hi in ((0, 8), (rows + 16, rows + 24)):
        shift_into(x4, w1, (4, 8, 12), wide, lo, hi)
    for b, lo in ((0, 0), (rows // 8 + 1, rows + 8)):
        second(b, 0)
        shift_into(x8, h2, (0, 8, 16), cols, lo, lo + 8)

    red_a = Reduce(bufs_a, me, counts)
    red_d = Reduce(bufs_d, me, counts)
    red_i = Reduce(bufs_i, me, counts)

    gc = jnp.zeros((classes, mid), F32)
    for b in range(rows // 8):
        a3 = nt(taps(x8, 8 * b, 8, 8), w8_ref[...])
        h3, s3v = act(a3)
        h3 = h3.astype(BF)
        expo = jnp.exp(nt(wc_ref[...], h3))
        prob = expo / jnp.sum(expo, axis=0, keepdims=True)
        label = jnp.concatenate(
            [
                jnp.broadcast_to(lab_ref[8 * b + j : 8 * b + j + 1, :], (classes, cols))
                for j in range(8)
            ],
            axis=1,
        )
        onehot = (label == lax.broadcasted_iota(jnp.int32, label.shape, 0)).astype(F32)
        g4 = (loss_weight * (prob - onehot)).astype(BF)
        gc = gc + nn(g4, h3)
        g3 = (tn(g4, wc_ref[...]) * s3v).astype(BF)
        w3[HALO + 8 * b : HALO + 8 * b + 8, SIDE : SIDE + cols, :] = g3.reshape(8, cols, mid)

    near2, far2 = halo(w3, 2, 0, 8), halo(w3, 3, 8, HALO - 8)
    near2.start()
    far2.start()

    def zero_tail(red, used):
        total = red.snd.shape[0]
        if total > used:
            red.snd[used:, :] = jnp.zeros((total - used, mid), BF)

    g3_t = flat2(w3[HALO : HALO + rows, SIDE : SIDE + cols, :]).T
    for ky in range(3):
        block = nn(g3_t, flat2(x8[8 * ky : 8 * ky + rows]))
        for kx in range(3):
            t = 3 * ky + kx
            red_a.snd[t * mid : (t + 1) * mid, :] = block[:, kx * mid : (kx + 1) * mid].astype(BF)
    red_a.snd[9 * mid : 9 * mid + classes, :] = gc.astype(BF)
    zero_tail(red_a, 9 * mid + classes)
    red_a.phase1()

    def third(base, count):
        back = nn(taps(xg, base, 8, count), wt8[...])
        grad = back.reshape(count, wide, mid) * s2[pl.ds(base + 4, count)]
        g2p[pl.ds(base, count)] = grad.astype(BF)

    near2.wait_recv()
    shift_into(xg, w3, (0, 8, 16), wide, 4, rows + 20)

    def third_own(b, _):
        third(8 * b + 4, 8)
        return 0

    lax.fori_loop(0, rows // 8, third_own, 0, unroll=True)
    red_a.phase2()

    spot = lax.broadcasted_iota(jnp.int32, (rows, wide, mid), 1)
    own = (spot >= 8) & (spot < 8 + cols)
    g2o[...] = jnp.where(own, g2p[4 : 4 + rows].astype(F32), 0.0).astype(BF)
    g2_t = flat2(g2o[...]).T
    for ky in range(3):
        block = nn(g2_t, flat2(x4[8 + 4 * ky : 8 + 4 * ky + rows]))
        for kx in range(3):
            t = 3 * ky + kx
            red_d.snd[t * mid : (t + 1) * mid, :] = block[:, kx * mid : (kx + 1) * mid].astype(BF)
    zero_tail(red_d, 9 * mid)
    red_d.phase1()
    red_a.phase3()
    shift_into(xg4, g2p, (4, 8, 12), cols, 4, rows + 4)

    far2.wait_recv()
    for lo in (0, rows + 20):
        shift_into(xg, w3, (0, 8, 16), wide, lo, lo + 4)
    for lo in (0, rows + 4):
        third(lo, 4)
        shift_into(xg4, g2p, (4, 8, 12), cols, lo, lo + 4)

    def fourth(b, _):
        back = nn(taps(xg4, 8 * b, 4, 8), wt4[...])
        s = flat2(s1[pl.ds(8 * b, 8)])
        g1[pl.ds(pl.multiple_of(b * 8 * cols, 128), 8 * cols), :] = (back * s).astype(BF)
        return 0

    lax.fori_loop(0, rows // 8, fourth, 0, unroll=True)
    red_d.phase2()
    gi = nn(flat_ref[...], g1[...])
    for k in range(chans // mid):
        block = gi[k * mid : (k + 1) * mid, :].T
        red_i.snd[k * mid : (k + 1) * mid, :] = block.astype(BF)
    zero_tail(red_i, chans)
    red_i.phase1()
    red_a.phase4()
    red_d.phase3()
    red_i.phase2()
    red_d.phase4()
    red_i.phase3()
    red_a.finish()
    for t in range(9):
        o8_ref[:, t * mid : (t + 1) * mid] = red_a.ag[t * mid : (t + 1) * mid, :]
    oc_ref[...] = red_a.ag[9 * mid : 9 * mid + classes, :]
    red_i.phase4()
    red_d.finish()
    for t in range(9):
        o4_ref[:, t * mid : (t + 1) * mid] = red_d.ag[t * mid : (t + 1) * mid, :]
    red_i.finish()
    for k in range(chans // mid):
        oi_ref[:, k * mid : (k + 1) * mid] = red_i.ag[k * mid : (k + 1) * mid, :]
    for item in (near1, far1, near2, far2):
        item.wait_send()
    for red in (red_a, red_d, red_i):
        red.drain()


def reduce_scratch(used, counts):
    nr, nc = counts
    unit = 16 * nr * nc
    total = -(-used // unit) * unit
    blk = total // nc
    piece = blk // nr
    sems = 2 * (nr - 1) + 2 * (nc - 1)
    return [
        pltpu.VMEM((total, 128), BF),
        pltpu.VMEM((max(nc - 1, 1), blk, 128), BF),
        pltpu.VMEM((blk, 128), BF),
        pltpu.VMEM((max(nr - 1, 1), piece, 128), BF),
        pltpu.VMEM((total, 128), BF),
        pltpu.SemaphoreType.DMA((sems,)),
        pltpu.SemaphoreType.DMA((sems,)),
    ]


def local(counts, features, labels, w_input, w_dilate4, w_dilate8, w_classes):
    chans, rows, cols = features.shape
    mid = w_input.shape[0]
    classes = w_classes.shape[0]
    wide = cols + 16
    flat = features.reshape(chans, rows * cols)
    vmem = pl.BlockSpec(memory_space=pltpu.VMEM)
    scratch = [
        pltpu.VMEM((rows + 24, cols + 32, mid), BF),
        pltpu.VMEM((rows + 24, wide, 3 * mid), BF),
        pltpu.VMEM((rows, cols, mid), F32),
        pltpu.VMEM((rows + 16, wide, mid), F32),
        pltpu.VMEM((rows + 16, wide, mid), BF),
        pltpu.VMEM((rows + 16, cols, 3 * mid), BF),
        pltpu.VMEM((rows + 24, cols + 32, mid), BF),
        pltpu.VMEM((rows + 24, wide, 3 * mid), BF),
        pltpu.VMEM((rows + 8, wide, mid), BF),
        pltpu.VMEM((rows, wide, mid), BF),
        pltpu.VMEM((rows + 8, cols, 3 * mid), BF),
        pltpu.VMEM((rows * cols, mid), BF),
        pltpu.VMEM((9 * mid, mid), BF),
        pltpu.VMEM((9 * mid, mid), BF),
    ]
    scratch += [pltpu.SemaphoreType.DMA((8,))] * 8
    scratch += reduce_scratch(9 * mid + classes, counts)
    scratch += reduce_scratch(9 * mid, counts)
    scratch += reduce_scratch(chans, counts)
    grads = pl.pallas_call(
        functools.partial(kernel, counts, rows, cols),
        out_shape=(
            jax.ShapeDtypeStruct((mid, chans), BF),
            jax.ShapeDtypeStruct((mid, 9 * mid), BF),
            jax.ShapeDtypeStruct((mid, 9 * mid), BF),
            jax.ShapeDtypeStruct((classes, mid), BF),
        ),
        in_specs=[vmem] * 6,
        out_specs=(vmem,) * 4,
        scratch_shapes=scratch,
        compiler_params=pltpu.CompilerParams(
            collective_id=0, has_side_effects=True, vmem_limit_bytes=56 * 1024 * 1024
        ),
        cost_estimate=pl.CostEstimate(
            flops=6_000_000_000, bytes_accessed=8_000_000, transcendentals=1_000_000
        ),
    )(flat, labels, w_input, w_dilate4, w_dilate8, w_classes)
    return tuple(grad.astype(F32) for grad in grads)


def solution(mesh):
    counts = (mesh.shape["rows"], mesh.shape["cols"])
    return jax.shard_map(
        functools.partial(local, counts),
        mesh=mesh,
        in_specs=(P(None, "rows", "cols"), P("rows", "cols"), P(), P(), P(), P()),
        out_specs=(P(), P(), P(), P()),
        check_vma=False,
    )
```
